32 devices in a mesh: dp: 8 (over y, x, core), tensor: 4 (over z).
Axes of the slice: x: 2, y: 2, z: 4, core: 2. Of those that a mesh axis runs over, the one named last changes fastest.
Arguments:
- hidden: bfloat16 [2048, 5120], P('dp', 'tensor'), may hold values from -6 to 6
- norm_gain: float32 [5120], replicated, may hold values from 0.1 to 1.9
- w_query: bfloat16 [5120, 8192], P(None, 'tensor'), may hold values from -0.078125 to 0.078125
- key_projection_weight: bfloat16 [5120, 1024], P(None, 'tensor'), may hold values from -0.078125 to 0.078125
- value_projection_weight: bfloat16 [5120, 1024], P(None, 'tensor'), may hold values from -0.078125 to 0.078125
- query_gain: float32 [128], replicated, may hold values from 1 to 4
- key_gain: float32 [128], replicated, may hold values from 0.5 to 2
- kv_pool: bfloat16 [3072, 8, 2, 16, 128], P(('dp', 'tensor')), may hold values from -102 to 102
- page_owner: int32 [8, 256], replicated, may hold values from 0 to 31, as said below
- page_slot: int32 [8, 256], replicated, may hold values from 0 to 95, as said below
- prefix_len: int32 [8], P('dp'), may hold values from 512 to 4096, as said below
- new_owner: int32 [8, 16, 1], P('dp'), may hold values from 0 to 7; in each aligned block of 16 rows (0 to 15, 16 to 31, ..., all dimensions but the last counted through in order) at most 2 rows name the same one
Outputs:
- attn_out: bfloat16 [2048, 8192], P('dp', 'tensor')
- fresh_page_store: bfloat16 [128, 8, 2, 16, 128], P('dp', 'tensor')
The draws below stay inside these ranges and needn't reach their ends.
Inputs may be any that keep to these rules, and one draw needn't show every extreme that they name: `page_owner`: for each request, no device owns more than 12 of its pages, and some device owns exactly 12. `page_slot`: the pages that one device owns sit in distinct slots. `prefix_len`: one request has the most cached tokens and one the least. `new_owner`: no dp index stores more than 2 new pages of one request.
All inputs are finite; a program needn't handle non-finite values.
Results may differ from the reference program's by a relative error of at most 0.006.
The reference program's roundings to bfloat16 on the way count: a program that leaves them out, or rounds other values in their place, can miss the bound.
Values may be sent and summed in bfloat16 or wider, within the bound.
A program may use at most 128 MiB of HBM per device.

```python
import math
import jax
import jax.numpy as jnp
import numpy as np
from jax import lax

MODEL_WIDTH = 5120
QUERY_HEADS = 64
KEY_VALUE_HEADS = 8
HEAD_SIZE = 128
PAGE_TOKENS = 16
SPAN = 256
NCAP = 2
MOST_PAGES = 256
FRESH_TOKENS = 2048
FRESH_PAGES = 16
CAP = 12
SLOTS = 96
POOL_SLOTS = 3072
STORE_SLOTS = 128
N_DP = 8
DEVICES = 32


def page_layout(key):
    reward_random_key, jitter_random_key, popular_random_key, ordering_random_key, placement_random_key = jax.random.split(key, 5)
    possible_owners = DEVICES * CAP
    possible_owner = jnp.arange(possible_owners, dtype=jnp.int32) // CAP
    extra_reward = jax.random.randint(reward_random_key, (N_DP, DEVICES), 0, 4096, dtype=jnp.int32)
    most_popular = jax.random.randint(popular_random_key, (N_DP,), 0, DEVICES, dtype=jnp.int32)
    extra_reward = jnp.where(jnp.arange(DEVICES, dtype=jnp.int32)[None, :] == most_popular[:, None], 8192, extra_reward)
    random_jitter = jax.random.randint(jitter_random_key, (N_DP, possible_owners), 0, 4096, dtype=jnp.int32)
    attention_scores = (random_jitter + extra_reward[:, possible_owner]) * possible_owners + jnp.arange(possible_owners, dtype=jnp.int32)[None, :]
    unused, chosen = lax.top_k(attention_scores, MOST_PAGES)
    shuffle_keys = jax.random.randint(ordering_random_key, (N_DP, MOST_PAGES), 0, 1 << 16, dtype=jnp.int32) * MOST_PAGES + jnp.arange(MOST_PAGES, dtype=jnp.int32)[None, :]
    order = jnp.argsort(shuffle_keys, axis=1)
    chosen = jnp.take_along_axis(chosen, order, axis=1).astype(jnp.int32)
    owners = chosen // CAP
    slot_keys = jax.random.randint(placement_random_key, (DEVICES, SLOTS), 0, 1 << 16, dtype=jnp.int32) * SLOTS + jnp.arange(SLOTS, dtype=jnp.int32)[None, :]
    arrangement = jnp.argsort(slot_keys, axis=1).astype(jnp.int32)
    local_index = jnp.arange(N_DP, dtype=jnp.int32)[:, None] * CAP + chosen % CAP
    slots = arrangement[owners, local_index]
    return (owners.astype(jnp.int32), slots.astype(jnp.int32))


def draw_page_owner(key, part):
    owners, slots = page_layout(key)
    return owners


def draw_page_slot(key, part):
    owners, slots = page_layout(key)
    return slots


def draw_prefix_len(key, part):
    key = jax.random.fold_in(key, 5)
    first_key, another_random_key = jax.random.split(key)
    longest = MOST_PAGES * PAGE_TOKENS
    shortest = longest // 8
    lengths = jax.random.randint(first_key, (N_DP,), shortest, longest + 1, dtype=jnp.int32)
    order = jax.random.permutation(another_random_key, N_DP)
    lengths = lengths.at[order[0]].set(longest).at[order[1]].set(shortest)
    return lengths.astype(jnp.int32)


def draw_kv_pool(key, part):
    key = jax.random.fold_in(key, 11)
    first_key = jax.random.fold_in(key, 0)
    array_dimensions = (POOL_SLOTS, KEY_VALUE_HEADS, 2, PAGE_TOKENS, HEAD_SIZE)
    base = jnp.clip(jax.random.normal(first_key, array_dimensions, jnp.float32), -6.0, 6.0)
    return base.astype(jnp.bfloat16)


def steps_of(stream_key, extent, cuts, smallest, largest):
    level, own = 1.0, jax.random.fold_in(stream_key, 6)
    for dim, shards_of in cuts:
        draws = jnp.exp(jax.random.uniform(jax.random.fold_in(own, dim), (shards_of,), jnp.float32, smallest / len(cuts), largest / len(cuts)))
        level = level * jnp.repeat(draws, extent[dim] // shards_of).reshape([-1 if axis == dim else 1 for axis in range(len(extent))])
    return level


def routed_block(rng, own, number, rows, number_of, top, most, slope):
    order = jax.random.permutation(rng, number_of)
    packed, common = shares(number_of, rows * top, most, slope, True), shares(number_of, rows * top, most, slope, False)
    places = jnp.arange(number_of)

    def named(sizes, offset_by):
        used = int((sizes > 0).sum())
        fixed = max(1, used // 4)
        passed = fixed + (places - fixed + offset_by * (used - fixed)) % max(1, number_of - fixed)
        return jnp.zeros((number_of,), jnp.int32).at[order[jnp.where(places < fixed, places, passed)]].set(jnp.asarray(sizes, jnp.int32))

    sizes = jnp.where(number % 4 == 0, named(packed, number // 4), named(common, number - number // 4 - 1))
    mixed = jax.random.permutation(jax.random.fold_in(own, 3), number_of)
    source_of, taker = mixed[0:number_of // 2 * 2:2], mixed[1:number_of // 2 * 2:2]
    slack = jnp.minimum(sizes[source_of] - 1, most - sizes[taker]) // 2
    slack = jnp.where((source_of == order[0]) | (taker == order[0]) | (sizes[taker] == 0), 0, jnp.maximum(slack, 0))
    passed = jax.random.randint(jax.random.fold_in(own, 4), (number_of // 2,), 0, 1 << 20) % (slack + 1)
    sizes = sizes.at[source_of].add(-passed).at[taker].add(passed)
    labels = jnp.searchsorted(jnp.cumsum(sizes), jnp.arange(rows * top), side="right").astype(jnp.int32)
    grid = labels.reshape(top, rows).T
    grid = grid[jax.random.permutation(jax.random.fold_in(own, 1), rows)]
    offset_by = jax.random.randint(jax.random.fold_in(own, 2), (rows, 1), 0, top)
    return jnp.take_along_axis(grid, (jnp.arange(top)[None, :] + offset_by) % top, axis=1)


def shares(number_of, total, reach, skew, full):
    loads = [(1 << 20) // math.isqrt(rank ** skew) + 1 for rank in range(1, number_of + 1)]
    largest = reach if full else min(reach, max(-(-total // number_of), total * loads[0] // sum(loads)))
    least = 1 if total - largest >= number_of - 1 else 0
    counts, surplus = [largest] + [least] * (number_of - 1), total - largest - least * (number_of - 1)
    while surplus > 0:
        candidates = [i for i in range(1, number_of) if counts[i] < largest] or [i for i in range(1, number_of) if counts[i] < reach]
        mass, remaining = sum([loads[i] for i in candidates]), surplus
        for i in candidates:
            addition = min(reach - counts[i], max(1, remaining * loads[i] // mass), surplus)
            counts[i] = counts[i] + addition
            surplus = surplus - addition
    return np.array(counts)


def bell_draw(key, shape, width, most, shards=(), kind=jnp.bfloat16):
    entries = width * jax.random.normal(key, shape, jnp.float32)
    if shards:
        entries = entries * steps_of(key, shape, shards, -0.22, 0.18)
    return jnp.clip(entries, -most, most).astype(kind)


def setup_inputs(seed: int = 0) -> dict:
    key_list = jax.random.split(jax.random.key(seed), 13)
    hidden = bell_draw(key_list[0], (FRESH_TOKENS, MODEL_WIDTH), 1.0, 6.0, ((0, 8), (1, 4)))
    norm_gain = jnp.clip(1.0 + 0.18 * jax.random.normal(key_list[1], (MODEL_WIDTH,), jnp.float32), 0.1, 1.9)
    w_query = bell_draw(key_list[2], (MODEL_WIDTH, QUERY_HEADS * HEAD_SIZE), MODEL_WIDTH ** -0.5, 0.078125, ((1, 4),))
    key_projection_weight = bell_draw(key_list[3], (MODEL_WIDTH, KEY_VALUE_HEADS * HEAD_SIZE), MODEL_WIDTH ** -0.5, 0.078125, ((1, 4),))
    value_projection_weight = bell_draw(key_list[4], (MODEL_WIDTH, KEY_VALUE_HEADS * HEAD_SIZE), MODEL_WIDTH ** -0.5, 0.078125, ((1, 4),))
    query_gain = jnp.clip(jnp.exp(jax.random.uniform(key_list[5], (HEAD_SIZE,), jnp.float32, math.log(1.0), math.log(4.0))), 1.0, 4.0)
    key_gain = jnp.clip(jnp.exp(jax.random.uniform(key_list[6], (HEAD_SIZE,), jnp.float32, math.log(0.5), math.log(2.0))), 0.5, 2.0)
    kv_pool = draw_kv_pool(jax.random.fold_in(key_list[12], 71), 0)
    page_owner = draw_page_owner(jax.random.fold_in(key_list[12], 71), 0)
    page_slot = draw_page_slot(jax.random.fold_in(key_list[12], 71), 0)
    prefix_len = draw_prefix_len(jax.random.fold_in(key_list[12], 71), 0)
    new_owner_keys = jax.random.split(jax.random.fold_in(key_list[11], 1), N_DP * FRESH_PAGES // FRESH_PAGES)
    new_owner_turns = jax.random.permutation(jax.random.fold_in(key_list[11], 3), N_DP * FRESH_PAGES // FRESH_PAGES)
    new_owner = jax.vmap(lambda own, number: routed_block(jax.random.fold_in(key_list[11], 2), own, number, FRESH_PAGES, N_DP, 1, NCAP, 1))(new_owner_keys, new_owner_turns).reshape((N_DP, FRESH_PAGES, 1))
    return {"hidden": hidden, "norm_gain": norm_gain, "w_query": w_query, "key_projection_weight": key_projection_weight, "value_projection_weight": value_projection_weight, "query_gain": query_gain, "key_gain": key_gain, "kv_pool": kv_pool, "page_owner": page_owner, "page_slot": page_slot, "prefix_len": prefix_len, "new_owner": new_owner}


EPS = 1e-06
THETA = 1000000.0
NEG = -1e+30

def rms_rows(values, gain):
    mean_square = lax.optimization_barrier(jnp.mean(values * values, axis=-1, keepdims=True))
    return values * lax.rsqrt(mean_square + EPS) * gain

def rotate(values, positions):
    half_width = values.shape[-1] // 2
    exponent = jnp.arange(half_width, dtype=jnp.float32) * (-2.0 / values.shape[-1])
    freqs = jnp.power(jnp.float32(THETA), exponent)
    angles = positions.astype(jnp.float32)[:, None] * freqs[None, :]
    cosine = jnp.cos(angles)[:, None, :]
    sine = jnp.sin(angles)[:, None, :]
    first_half = values[..., :half_width]
    second_half = values[..., half_width:]
    return jnp.concatenate([first_half * cosine - second_half * sine, second_half * cosine + first_half * sine], axis=-1)

def reference(hidden, norm_gain, w_query, key_projection_weight, value_projection_weight, query_gain, key_gain, kv_pool, page_owner, page_slot, prefix_len, new_owner):
    scale = 1.0 / math.sqrt(HEAD_SIZE)
    heads_per_group = QUERY_HEADS // KEY_VALUE_HEADS
    normalized_rows = rms_rows(hidden.astype(jnp.float32), norm_gain).astype(jnp.bfloat16)
    offsets = jnp.arange(SPAN, dtype=jnp.int32)
    positions = (prefix_len[:, None] + offsets[None, :]).reshape(FRESH_TOKENS).astype(jnp.int32)
    query_flat = jnp.dot(normalized_rows, w_query, preferred_element_type=jnp.float32).reshape(FRESH_TOKENS, QUERY_HEADS, HEAD_SIZE)
    flattened_keys = jnp.dot(normalized_rows, key_projection_weight, preferred_element_type=jnp.float32).reshape(FRESH_TOKENS, KEY_VALUE_HEADS, HEAD_SIZE)
    queries = rotate(rms_rows(query_flat, query_gain), positions).astype(jnp.bfloat16)
    new_keys = rotate(rms_rows(flattened_keys, key_gain), positions).astype(jnp.bfloat16)
    fresh_value_rows = jnp.dot(normalized_rows, value_projection_weight, preferred_element_type=jnp.float32).astype(jnp.bfloat16).reshape(FRESH_TOKENS, KEY_VALUE_HEADS, HEAD_SIZE)
    causal = offsets[:, None] >= offsets[None, :]

    def one_request(request):
        owners = lax.dynamic_index_in_dim(page_owner, request, 0, keepdims=False)
        slots = lax.dynamic_index_in_dim(page_slot, request, 0, keepdims=False)
        length = lax.dynamic_index_in_dim(prefix_len, request, 0, keepdims=False)
        cached_pages = jnp.take(kv_pool, owners * SLOTS + slots, axis=0)
        stored_key_rows = cached_pages[:, :, 0].transpose(1, 0, 2, 3).reshape(KEY_VALUE_HEADS, MOST_PAGES * PAGE_TOKENS, HEAD_SIZE)
        stored_value_rows = cached_pages[:, :, 1].transpose(1, 0, 2, 3).reshape(KEY_VALUE_HEADS, MOST_PAGES * PAGE_TOKENS, HEAD_SIZE)
        live = jnp.arange(MOST_PAGES * PAGE_TOKENS, dtype=jnp.int32) < length
        start = (request * SPAN).astype(jnp.int32)
        query_rows = lax.dynamic_slice_in_dim(queries, start, SPAN, 0)
        key_rows = lax.dynamic_slice_in_dim(new_keys, start, SPAN, 0)
        value_rows = lax.dynamic_slice_in_dim(fresh_value_rows, start, SPAN, 0)

        def one_head(head):
            kv_index = head // heads_per_group
            query_head = lax.dynamic_index_in_dim(query_rows, head, 1, keepdims=False)
            prior_keys = lax.dynamic_index_in_dim(stored_key_rows, kv_index, 0, keepdims=False)
            prior_values = lax.dynamic_index_in_dim(stored_value_rows, kv_index, 0, keepdims=False)
            span_keys = lax.dynamic_index_in_dim(key_rows, kv_index, 1, keepdims=False)
            span_values = lax.dynamic_index_in_dim(value_rows, kv_index, 1, keepdims=False)
            prior = jnp.dot(query_head, prior_keys.T, preferred_element_type=jnp.float32) * scale
            prior = jnp.where(live[None, :], prior, NEG)
            recent = jnp.dot(query_head, span_keys.T, preferred_element_type=jnp.float32) * scale
            recent = jnp.where(causal, recent, NEG)
            peak = jnp.maximum(lax.optimization_barrier(jnp.max(prior, axis=1)), lax.optimization_barrier(jnp.max(recent, axis=1)))[:, None]
            prior_exp = jnp.exp(prior - peak)
            recent_exp = jnp.exp(recent - peak)
            total = lax.optimization_barrier(jnp.sum(prior_exp, axis=1)) + lax.optimization_barrier(jnp.sum(recent_exp, axis=1))
            mixed = jnp.dot(prior_exp.astype(jnp.bfloat16), prior_values, preferred_element_type=jnp.float32)
            mixed = mixed + jnp.dot(recent_exp.astype(jnp.bfloat16), span_values, preferred_element_type=jnp.float32)
            return (mixed / total[:, None]).astype(jnp.bfloat16)
        heads_out = lax.map(one_head, jnp.arange(QUERY_HEADS, dtype=jnp.int32))
        return heads_out.transpose(1, 0, 2).reshape(SPAN, QUERY_HEADS * HEAD_SIZE)
    attn_out = lax.map(one_request, jnp.arange(N_DP, dtype=jnp.int32)).reshape(FRESH_TOKENS, QUERY_HEADS * HEAD_SIZE)
    targets = new_owner[:, :, 0]
    page_index = jnp.arange(FRESH_PAGES, dtype=jnp.int32)
    earlier = page_index[None, :] < page_index[:, None]
    same_owner = targets[:, :, None] == targets[:, None, :]
    ranks = lax.optimization_barrier(jnp.sum(same_owner & earlier[None], axis=2)).astype(jnp.int32)
    target_owner = targets * (N_DP * NCAP) + jnp.arange(N_DP, dtype=jnp.int32)[:, None] * NCAP + ranks
    stacked_pages = jnp.stack([new_keys, fresh_value_rows], axis=2)
    fresh_pages = stacked_pages.reshape(N_DP, FRESH_PAGES, PAGE_TOKENS, KEY_VALUE_HEADS, 2, HEAD_SIZE).transpose(0, 1, 3, 4, 2, 5).reshape(N_DP * FRESH_PAGES, KEY_VALUE_HEADS, 2, PAGE_TOKENS, HEAD_SIZE)
    fresh_page_store = jnp.zeros((STORE_SLOTS, KEY_VALUE_HEADS, 2, PAGE_TOKENS, HEAD_SIZE), jnp.bfloat16).at[target_owner.reshape(N_DP * FRESH_PAGES)].set(fresh_pages)
    return (attn_out, fresh_page_store)
```

```python
import functools
import math

import jax
import jax.numpy as jnp
from jax import lax
from jax.experimental import pallas as pl
from jax.experimental.pallas import tpu as pltpu
from jax.sharding import PartitionSpec as P

HEAD_SIZE = 128
PAGE_TOKENS = 16
SPAN = 256
NCAP = 2
MOST_PAGES = 256


EPS = 1e-06
THETA = 1000000.0
NEG = -1e30


def rms_rows(values, gain):
    mean_square = jnp.mean(values * values, axis=-1, keepdims=True)
    return values * lax.rsqrt(mean_square + EPS) * gain


def rotate(values, positions):
    half_width = values.shape[-1] // 2
    exponent = jnp.arange(half_width, dtype=jnp.float32) * (-2.0 / values.shape[-1])
    freqs = jnp.power(jnp.float32(THETA), exponent)
    angles = positions.astype(jnp.float32)[:, None] * freqs[None, :]
    cosine = jnp.cos(angles)[:, None, :]
    sine = jnp.sin(angles)[:, None, :]
    first_half = values[..., :half_width]
    second_half = values[..., half_width:]
    return jnp.concatenate(
        [first_half * cosine - second_half * sine, second_half * cosine + first_half * sine],
        axis=-1,
    )


def collect(matches, payload, capacity):
    ranks = jnp.cumsum(matches.astype(jnp.int32), axis=1) - 1
    places = jnp.arange(capacity, dtype=jnp.int32)
    landed = matches[:, :, None] & (ranks[:, :, None] == places[None, None, :])
    picked = jnp.sum(jnp.where(landed, payload[:, :, None], 0), axis=1)
    return (picked, jnp.any(landed, axis=1))


def gather_kernel(key_heads, rows, capacity, picked_ref, pool_ref, *refs):
    outs, sem = refs[:key_heads], refs[key_heads]

    def send(n, carry):
        r = n // capacity
        c = n - r * capacity
        slot = picked_ref[n]
        for h in range(key_heads):
            pltpu.make_async_copy(
                pool_ref.at[slot, :, h], outs[h].at[r, :, c], sem.at[h]
            ).start()
        return carry

    lax.fori_loop(0, rows * capacity, send, 0)
    for h in range(key_heads):
        pltpu.make_async_copy(outs[h], outs[h], sem.at[h]).wait()


def gather_pages(picked, pool, key_heads):
    rows, capacity = picked.shape
    slots, groups = pool.shape[0], pool.shape[1] // key_heads
    split_pool = pool.reshape((slots, groups, key_heads) + pool.shape[2:])
    out = jax.ShapeDtypeStruct((rows, groups, capacity) + pool.shape[2:], pool.dtype)
    return pl.pallas_call(
        functools.partial(gather_kernel, key_heads, rows, capacity),
        out_shape=[out] * key_heads,
        in_specs=[
            pl.BlockSpec(memory_space=pltpu.SMEM),
            pl.BlockSpec(memory_space=pl.ANY),
        ],
        out_specs=[pl.BlockSpec(memory_space=pl.ANY)] * key_heads,
        scratch_shapes=[pltpu.SemaphoreType.DMA((key_heads,))],
        name="gather_pages",
    )(picked.reshape(-1), split_pool)


BLOCK_PAGES = 32
ROW_TILES = 2


def attention_kernel(
    group, scale, places_ref, length_ref, q_ref, k_ref, v_ref, pages_ref, *refs
):
    out_ref, keys, values, acc, top = refs[-5:]
    length = length_ref[0]
    columns = BLOCK_PAGES * PAGE_TOKENS
    live_pages = (length + PAGE_TOKENS - 1) // PAGE_TOKENS
    full = length // columns
    blocks = (length + columns - 1) // columns
    ones = jnp.ones((PAGE_TOKENS, HEAD_SIZE), jnp.bfloat16)
    factor = scale * math.log2(math.e)

    def place(i, carry):
        for u in range(8):
            j = i * 8 + u
            at = places_ref[j]
            keys[j] = pages_ref[at, 0]
            values[j, :, :HEAD_SIZE] = pages_ref[at, 1]
            values[j, :, HEAD_SIZE:] = ones
        return carry

    lax.fori_loop(0, (live_pages + 7) // 8, place, 0)

    def spare(j, carry):
        values[j] = jnp.zeros(values.shape[1:], jnp.bfloat16)
        keys[j] = jnp.zeros(keys.shape[1:], jnp.bfloat16)
        return carry

    lax.fori_loop((live_pages + 7) // 8 * 8, blocks * BLOCK_PAGES, spare, 0)
    rows = q_ref.shape[0]
    row_ids = lax.broadcasted_iota(jnp.int32, (rows, rows), 0)
    column_ids = lax.broadcasted_iota(jnp.int32, (rows, rows), 1)
    causal = row_ids >= column_ids
    span_keys = k_ref[...]
    span_values = jnp.concatenate(
        [v_ref[...], jnp.ones((rows, HEAD_SIZE), jnp.bfloat16)], axis=1
    )
    contract_last = (((1,), (1,)), ((), ()))

    def scores_of(query, key_rows):
        return (
            lax.dot_general(query, key_rows, contract_last, preferred_element_type=jnp.float32)
            * factor
        )

    for g in range(0, group, ROW_TILES):
        queries = [q_ref[:, (g + t) * HEAD_SIZE : (g + t + 1) * HEAD_SIZE] for t in range(ROW_TILES)]
        for t in range(ROW_TILES):
            recent = jnp.where(causal, scores_of(queries[t], span_keys), NEG)
            peak = jnp.max(recent, axis=1, keepdims=True)
            weights = jnp.exp2(recent - peak).astype(jnp.bfloat16)
            top[t] = jnp.broadcast_to(peak, (rows, HEAD_SIZE))
            acc[t] = jnp.dot(weights, span_values, preferred_element_type=jnp.float32)

        def step(i, masked):
            start = pl.multiple_of(i * BLOCK_PAGES, BLOCK_PAGES)
            key_rows = keys[pl.ds(start, BLOCK_PAGES)].reshape(columns, HEAD_SIZE)
            value_rows = values[pl.ds(start, BLOCK_PAGES)].reshape(columns, 2 * HEAD_SIZE)
            for t in range(ROW_TILES):
                scores = scores_of(queries[t], key_rows)
                if masked:
                    positions = i * columns + lax.broadcasted_iota(jnp.int32, scores.shape, 1)
                    scores = jnp.where(positions < length, scores, NEG)
                before = top[t][:, :1]
                peak = jnp.maximum(before, jnp.max(scores, axis=1, keepdims=True))
                weights = jnp.exp2(scores - peak).astype(jnp.bfloat16)
                acc[t] = acc[t] * jnp.exp2(before - peak) + jnp.dot(
                    weights, value_rows, preferred_element_type=jnp.float32
                )
                top[t] = jnp.broadcast_to(peak, (rows, HEAD_SIZE))

        lax.fori_loop(0, full, lambda i, c: (step(i, False), c)[1], 0)

        @pl.when(full < blocks)
        def _():
            step(full, True)

        for t in range(ROW_TILES):
            mixed = acc[t]
            out_ref[:, (g + t) * HEAD_SIZE : (g + t + 1) * HEAD_SIZE] = (
                mixed[:, :HEAD_SIZE] / mixed[:, HEAD_SIZE:]
            ).astype(jnp.bfloat16)


def attend(places, prefix_len, queries, new_keys, new_values, pages, h, key_heads, out, scale):
    rows, width = queries.shape
    part = width // key_heads
    group = part // HEAD_SIZE
    most = places.shape[0]
    vmem = lambda block, index: pl.BlockSpec(block, index)
    in_specs = [
        pl.BlockSpec(memory_space=pltpu.SMEM),
        pl.BlockSpec(memory_space=pltpu.SMEM),
        vmem((rows, part), lambda i: (0, h)),
        vmem((rows, HEAD_SIZE), lambda i: (0, h)),
        vmem((rows, HEAD_SIZE), lambda i: (0, h)),
        vmem(pages.shape, lambda i: (0,) * pages.ndim),
    ]
    operands = [places, prefix_len, queries, new_keys, new_values, pages]
    aliases = {}
    if out is not None:
        in_specs.append(pl.BlockSpec(memory_space=pl.ANY))
        operands.append(out)
        aliases = {len(operands) - 1: 0}
    return pl.pallas_call(
        functools.partial(attention_kernel, group, scale),
        grid=(1,),
        out_shape=jax.ShapeDtypeStruct((rows, width), jnp.bfloat16),
        in_specs=in_specs,
        out_specs=vmem((rows, part), lambda i: (0, h)),
        scratch_shapes=[
            pltpu.VMEM((most, PAGE_TOKENS, HEAD_SIZE), jnp.bfloat16),
            pltpu.VMEM((most, PAGE_TOKENS, 2 * HEAD_SIZE), jnp.bfloat16),
            pltpu.VMEM((ROW_TILES, rows, 2 * HEAD_SIZE), jnp.float32),
            pltpu.VMEM((ROW_TILES, rows, HEAD_SIZE), jnp.float32),
        ],
        input_output_aliases=aliases,
        compiler_params=pltpu.CompilerParams(vmem_limit_bytes=40 * 2**20),
        cost_estimate=pl.CostEstimate(
            flops=4 * rows * part * most * PAGE_TOKENS,
            bytes_accessed=2 * pages.size,
            transcendentals=rows * group * most * PAGE_TOKENS,
        ),
        name="attend_head",
    )(*operands)


def shards(
    hidden,
    norm_gain,
    w_query,
    key_projection_weight,
    value_projection_weight,
    query_gain,
    key_gain,
    kv_pool,
    page_owner,
    page_slot,
    prefix_len,
    new_owner,
):
    data_ways = lax.axis_size("dp")
    tensor_ways = lax.axis_size("tensor")
    request = lax.axis_index("dp")
    slot_count = kv_pool.shape[0]
    capacity = slot_count // data_ways
    key_heads = key_projection_weight.shape[1] // HEAD_SIZE
    local_heads = w_query.shape[1] // HEAD_SIZE
    scale = 1.0 / math.sqrt(HEAD_SIZE)
    full_rows = lax.all_gather(hidden, "tensor", axis=1, tiled=True)
    normalized_rows = rms_rows(full_rows.astype(jnp.float32), norm_gain).astype(jnp.bfloat16)
    length = prefix_len[0]
    offsets = jnp.arange(SPAN, dtype=jnp.int32)
    positions = length + offsets
    query_flat = jnp.dot(normalized_rows, w_query, preferred_element_type=jnp.float32).reshape(
        SPAN, local_heads, HEAD_SIZE
    )
    flattened_keys = jnp.dot(
        normalized_rows, key_projection_weight, preferred_element_type=jnp.float32
    ).reshape(SPAN, key_heads, HEAD_SIZE)
    queries = rotate(rms_rows(query_flat, query_gain), positions).astype(jnp.bfloat16)
    new_keys = rotate(rms_rows(flattened_keys, key_gain), positions).astype(jnp.bfloat16)
    fresh_value_rows = (
        jnp.dot(normalized_rows, value_projection_weight, preferred_element_type=jnp.float32)
        .astype(jnp.bfloat16)
        .reshape(SPAN, key_heads, HEAD_SIZE)
    )
    page_count = SPAN // PAGE_TOKENS
    stacked_pages = jnp.stack([new_keys, fresh_value_rows], axis=2)
    fresh_pages = (
        stacked_pages.reshape(page_count, PAGE_TOKENS, key_heads, 2, HEAD_SIZE)
        .transpose(0, 2, 3, 1, 4)
        .reshape(page_count, key_heads * 2 * PAGE_TOKENS * HEAD_SIZE)
    )
    targets = new_owner[0, :, 0]
    page_index = jnp.arange(page_count, dtype=jnp.int32)
    earlier = page_index[None, :] < page_index[:, None]
    ranks = jnp.sum((targets[:, None] == targets[None, :]) & earlier, axis=1)
    slot_index = jnp.arange(data_ways * NCAP, dtype=jnp.int32)
    selector = ((targets * NCAP + ranks)[None, :] == slot_index[:, None]).astype(jnp.bfloat16)
    outgoing_pages = jnp.dot(selector, fresh_pages, preferred_element_type=jnp.float32).astype(
        jnp.bfloat16
    )
    outgoing_pages = outgoing_pages.reshape(data_ways * NCAP, key_heads, 2, PAGE_TOKENS, HEAD_SIZE)
    fresh_page_store = lax.all_to_all(outgoing_pages, "dp", split_axis=0, concat_axis=0, tiled=True)
    own_row = lax.dynamic_index_in_dim(page_owner, request, 0, keepdims=False)
    my_device = request * tensor_ways + lax.axis_index("tensor")
    picked, unused = collect(page_owner == my_device, page_slot, capacity)
    outgoing = gather_pages(picked, kv_pool, key_heads)
    sources = data_ways * tensor_ways
    arrived = [
        lax.all_to_all(
            pages.reshape((sources, capacity) + pages.shape[3:]),
            ("dp", "tensor"),
            split_axis=0,
            concat_axis=0,
            tiled=True,
        ).reshape((sources * capacity,) + pages.shape[3:])
        for pages in outgoing
    ]
    same = own_row[:, None] == own_row[None, :]
    later = jnp.arange(MOST_PAGES)[:, None] > jnp.arange(MOST_PAGES)[None, :]
    places = own_row * capacity + jnp.sum(same & later, axis=1).astype(jnp.int32)
    attn_out = None
    for h in range(key_heads):
        attn_out = attend(
            places,
            prefix_len,
            queries.reshape(SPAN, local_heads * HEAD_SIZE),
            new_keys.reshape(SPAN, key_heads * HEAD_SIZE),
            fresh_value_rows.reshape(SPAN, key_heads * HEAD_SIZE),
            arrived[h],
            h,
            key_heads,
            attn_out,
            scale,
        )
    return (attn_out, fresh_page_store)


def solution(mesh):
    return jax.shard_map(
        shards,
        mesh=mesh,
        in_specs=(
            P("dp", "tensor"),
            P(),
            P(None, "tensor"),
            P(None, "tensor"),
            P(None, "tensor"),
            P(),
            P(),
            P(("dp", "tensor"), None, None, None, None),
            P(),
            P(),
            P("dp"),
            P("dp", None, None),
        ),
        out_specs=(P("dp", "tensor"), P("dp", "tensor", None, None, None)),
        check_vma=False,
    )
```

```python
import functools
import math

import jax
import jax.numpy as jnp
from jax import lax
from jax.experimental import pallas as pl
from jax.experimental.pallas import tpu as pltpu
from jax.sharding import PartitionSpec as P

HEAD_SIZE = 128
PAGE_TOKENS = 16
SPAN = 256
NCAP = 2
MOST_PAGES = 256


EPS = 1e-06
THETA = 1000000.0
NEG = -1e30


def rms_rows(values, gain):
    mean_square = jnp.mean(values * values, axis=-1, keepdims=True)
    return values * lax.rsqrt(mean_square + EPS) * gain


def rotate(values, positions):
    half_width = values.shape[-1] // 2
    exponent = jnp.arange(half_width, dtype=jnp.float32) * (-2.0 / values.shape[-1])
    freqs = jnp.power(jnp.float32(THETA), exponent)
    angles = positions.astype(jnp.float32)[:, None] * freqs[None, :]
    cosine = jnp.cos(angles)[:, None, :]
    sine = jnp.sin(angles)[:, None, :]
    first_half = values[..., :half_width]
    second_half = values[..., half_width:]
    return jnp.concatenate(
        [first_half * cosine - second_half * sine, second_half * cosine + first_half * sine],
        axis=-1,
    )


def collect(matches, payload, capacity):
    ranks = jnp.cumsum(matches.astype(jnp.int32), axis=1) - 1
    places = jnp.arange(capacity, dtype=jnp.int32)
    landed = matches[:, :, None] & (ranks[:, :, None] == places[None, None, :])
    picked = jnp.sum(jnp.where(landed, payload[:, :, None], 0), axis=1)
    return (picked, jnp.any(landed, axis=1))


def gather_kernel(key_heads, groups, capacity, picked_ref, pool_ref, *outs):
    row = pl.program_id(0)

    def pick(c, carry):
        slot = picked_ref[row * capacity + c]
        for h in range(key_heads):
            for t in range(groups):
                outs[h][0, t, c] = pool_ref[slot, t * key_heads + h]
        return carry

    lax.fori_loop(0, capacity, pick, 0)


def gather_pages(picked, pool, key_heads):
    rows, capacity = picked.shape
    groups = pool.shape[1] // key_heads
    page = pool.shape[2:]
    out = jax.ShapeDtypeStruct((rows, groups, capacity) + page, pool.dtype)
    block = pl.BlockSpec((1, groups, capacity) + page, lambda r: (r, 0, 0, 0, 0, 0))
    return pl.pallas_call(
        functools.partial(gather_kernel, key_heads, groups, capacity),
        grid=(rows,),
        out_shape=[out] * key_heads,
        in_specs=[
            pl.BlockSpec(memory_space=pltpu.SMEM),
            pl.BlockSpec(memory_space=pltpu.VMEM),
        ],
        out_specs=[block] * key_heads,
        compiler_params=pltpu.CompilerParams(vmem_limit_bytes=32 * 2**20),
        cost_estimate=pl.CostEstimate(flops=0, bytes_accessed=4 * pool.size, transcendentals=0),
        name="gather_pages",
    )(picked.reshape(-1), pool)


BLOCK_PAGES = 128
ROW_TILES = 8


def attention_kernel(
    group, scale, places_ref, length_ref, q_ref, k_ref, v_ref, pages_ref, *refs
):
    out_ref, keys, values, acc, top = refs[-5:]
    length = length_ref[0]
    columns = BLOCK_PAGES * PAGE_TOKENS
    live_pages = (length + PAGE_TOKENS - 1) // PAGE_TOKENS
    full = length // columns
    blocks = (length + columns - 1) // columns
    ones = jnp.ones((PAGE_TOKENS, HEAD_SIZE), jnp.bfloat16)
    factor = scale * math.log2(math.e)

    def place(i, carry):
        for u in range(8):
            j = i * 8 + u
            at = places_ref[j]
            keys[j] = pages_ref[at, 0]
            values[j, :, :HEAD_SIZE] = pages_ref[at, 1]
            values[j, :, HEAD_SIZE:] = ones
        return carry

    lax.fori_loop(0, (live_pages + 7) // 8, place, 0)

    def spare(j, carry):
        values[j] = jnp.zeros(values.shape[1:], jnp.bfloat16)
        keys[j] = jnp.zeros(keys.shape[1:], jnp.bfloat16)
        return carry

    lax.fori_loop((live_pages + 7) // 8 * 8, blocks * BLOCK_PAGES, spare, 0)
    rows = q_ref.shape[0]
    row_ids = lax.broadcasted_iota(jnp.int32, (rows, rows), 0)
    column_ids = lax.broadcasted_iota(jnp.int32, (rows, rows), 1)
    causal = row_ids >= column_ids
    span_keys = k_ref[...]
    span_values = jnp.concatenate(
        [v_ref[...], jnp.ones((rows, HEAD_SIZE), jnp.bfloat16)], axis=1
    )
    contract_last = (((1,), (1,)), ((), ()))

    def scores_of(query, key_rows):
        return (
            lax.dot_general(query, key_rows, contract_last, preferred_element_type=jnp.float32)
            * factor
        )

    for g in range(0, group, ROW_TILES):
        queries = [q_ref[:, (g + t) * HEAD_SIZE : (g + t + 1) * HEAD_SIZE] for t in range(ROW_TILES)]
        for t in range(ROW_TILES):
            recent = jnp.where(causal, scores_of(queries[t], span_keys), NEG)
            peak = jnp.max(recent, axis=1, keepdims=True)
            weights = jnp.exp2(recent - peak).astype(jnp.bfloat16)
            top[t] = jnp.broadcast_to(peak, (rows, HEAD_SIZE))
            acc[t] = jnp.dot(weights, span_values, preferred_element_type=jnp.float32)

        def step(i, masked):
            start = pl.multiple_of(i * BLOCK_PAGES, BLOCK_PAGES)
            key_rows = keys[pl.ds(start, BLOCK_PAGES)].reshape(columns, HEAD_SIZE)
            value_rows = values[pl.ds(start, BLOCK_PAGES)].reshape(columns, 2 * HEAD_SIZE)
            for t in range(ROW_TILES):
                scores = scores_of(queries[t], key_rows)
                if masked:
                    positions = i * columns + lax.broadcasted_iota(jnp.int32, scores.shape, 1)
                    scores = jnp.where(positions < length, scores, NEG)
                before = top[t][:, :1]
                peak = jnp.maximum(before, jnp.max(scores, axis=1, keepdims=True))
                weights = jnp.exp2(scores - peak).astype(jnp.bfloat16)
                acc[t] = acc[t] * jnp.exp2(before - peak) + jnp.dot(
                    weights, value_rows, preferred_element_type=jnp.float32
                )
                top[t] = jnp.broadcast_to(peak, (rows, HEAD_SIZE))

        lax.fori_loop(0, full, lambda i, c: (step(i, False), c)[1], 0)

        @pl.when(full < blocks)
        def _():
            step(full, True)

        for t in range(ROW_TILES):
            mixed = acc[t]
            out_ref[:, (g + t) * HEAD_SIZE : (g + t + 1) * HEAD_SIZE] = (
                mixed[:, :HEAD_SIZE] / mixed[:, HEAD_SIZE:]
            ).astype(jnp.bfloat16)


def attend(places, prefix_len, queries, new_keys, new_values, pages, h, key_heads, out, scale):
    rows, width = queries.shape
    part = width // key_heads
    group = part // HEAD_SIZE
    most = places.shape[0]
    vmem = lambda block, index: pl.BlockSpec(block, index)
    in_specs = [
        pl.BlockSpec(memory_space=pltpu.SMEM),
        pl.BlockSpec(memory_space=pltpu.SMEM),
        vmem((rows, part), lambda i: (0, h)),
        vmem((rows, HEAD_SIZE), lambda i: (0, h)),
        vmem((rows, HEAD_SIZE), lambda i: (0, h)),
        vmem(pages.shape, lambda i: (0,) * pages.ndim),
    ]
    operands = [places, prefix_len, queries, new_keys, new_values, pages]
    aliases = {}
    if out is not None:
        in_specs.append(pl.BlockSpec(memory_space=pl.ANY))
        operands.append(out)
        aliases = {len(operands) - 1: 0}
    return pl.pallas_call(
        functools.partial(attention_kernel, group, scale),
        grid=(1,),
        out_shape=jax.ShapeDtypeStruct((rows, width), jnp.bfloat16),
        in_specs=in_specs,
        out_specs=vmem((rows, part), lambda i: (0, h)),
        scratch_shapes=[
            pltpu.VMEM((most, PAGE_TOKENS, HEAD_SIZE), jnp.bfloat16),
            pltpu.VMEM((most, PAGE_TOKENS, 2 * HEAD_SIZE), jnp.bfloat16),
            pltpu.VMEM((ROW_TILES, rows, 2 * HEAD_SIZE), jnp.float32),
            pltpu.VMEM((ROW_TILES, rows, HEAD_SIZE), jnp.float32),
        ],
        input_output_aliases=aliases,
        compiler_params=pltpu.CompilerParams(vmem_limit_bytes=40 * 2**20),
        cost_estimate=pl.CostEstimate(
            flops=4 * rows * part * most * PAGE_TOKENS,
            bytes_accessed=2 * pages.size,
            transcendentals=rows * group * most * PAGE_TOKENS,
        ),
        name="attend_head",
    )(*operands)


def shards(
    hidden,
    norm_gain,
    w_query,
    key_projection_weight,
    value_projection_weight,
    query_gain,
    key_gain,
    kv_pool,
    page_owner,
    page_slot,
    prefix_len,
    new_owner,
):
    data_ways = lax.axis_size("dp")
    tensor_ways = lax.axis_size("tensor")
    request = lax.axis_index("dp")
    slot_count = kv_pool.shape[0]
    capacity = slot_count // data_ways
    key_heads = key_projection_weight.shape[1] // HEAD_SIZE
    local_heads = w_query.shape[1] // HEAD_SIZE
    scale = 1.0 / math.sqrt(HEAD_SIZE)
    own_row = lax.dynamic_index_in_dim(page_owner, request, 0, keepdims=False)
    my_device = request * tensor_ways + lax.axis_index("tensor")
    picked, unused = collect(page_owner == my_device, page_slot, capacity)
    outgoing = gather_pages(picked, kv_pool, key_heads)
    sources = data_ways * tensor_ways
    arrived = []
    for pages in outgoing:
        if arrived:
            pages, arrived[-1] = lax.optimization_barrier((pages, arrived[-1]))
        arrived.append(
            lax.all_to_all(
                pages.reshape((sources, capacity) + pages.shape[3:]),
                ("dp", "tensor"),
                split_axis=0,
                concat_axis=0,
                tiled=True,
            ).reshape((sources * capacity,) + pages.shape[3:])
        )
    full_rows = lax.all_gather(hidden, "tensor", axis=1, tiled=True)
    full_rows, outgoing = lax.optimization_barrier((full_rows, outgoing))
    normalized_rows = rms_rows(full_rows.astype(jnp.float32), norm_gain).astype(jnp.bfloat16)
    length = prefix_len[0]
    offsets = jnp.arange(SPAN, dtype=jnp.int32)
    positions = length + offsets
    query_flat = jnp.dot(normalized_rows, w_query, preferred_element_type=jnp.float32).reshape(
        SPAN, local_heads, HEAD_SIZE
    )
    flattened_keys = jnp.dot(
        normalized_rows, key_projection_weight, preferred_element_type=jnp.float32
    ).reshape(SPAN, key_heads, HEAD_SIZE)
    queries = rotate(rms_rows(query_flat, query_gain), positions).astype(jnp.bfloat16)
    new_keys = rotate(rms_rows(flattened_keys, key_gain), positions).astype(jnp.bfloat16)
    fresh_value_rows = (
        jnp.dot(normalized_rows, value_projection_weight, preferred_element_type=jnp.float32)
        .astype(jnp.bfloat16)
        .reshape(SPAN, key_heads, HEAD_SIZE)
    )
    page_count = SPAN // PAGE_TOKENS
    stacked_pages = jnp.stack([new_keys, fresh_value_rows], axis=2)
    fresh_pages = (
        stacked_pages.reshape(page_count, PAGE_TOKENS, key_heads, 2, HEAD_SIZE)
        .transpose(0, 2, 3, 1, 4)
        .reshape(page_count, key_heads * 2 * PAGE_TOKENS * HEAD_SIZE)
    )
    targets = new_owner[0, :, 0]
    page_index = jnp.arange(page_count, dtype=jnp.int32)
    earlier = page_index[None, :] < page_index[:, None]
    ranks = jnp.sum((targets[:, None] == targets[None, :]) & earlier, axis=1)
    slot_index = jnp.arange(data_ways * NCAP, dtype=jnp.int32)
    selector = ((targets * NCAP + ranks)[None, :] == slot_index[:, None]).astype(jnp.bfloat16)
    outgoing_pages = jnp.dot(selector, fresh_pages, preferred_element_type=jnp.float32).astype(
        jnp.bfloat16
    )
    outgoing_pages = outgoing_pages.reshape(data_ways * NCAP, key_heads, 2, PAGE_TOKENS, HEAD_SIZE)
    outgoing_pages = outgoing_pages.reshape(
        (data_ways, NCAP) + outgoing_pages.shape[1:]
    )
    every = lax.all_gather(outgoing_pages, "dp", axis=0)
    fresh_page_store = lax.dynamic_index_in_dim(every, request, 1, keepdims=False)
    fresh_page_store = fresh_page_store.reshape((data_ways * NCAP,) + outgoing_pages.shape[2:])
    same = own_row[:, None] == own_row[None, :]
    later = jnp.arange(MOST_PAGES)[:, None] > jnp.arange(MOST_PAGES)[None, :]
    places = own_row * capacity + jnp.sum(same & later, axis=1).astype(jnp.int32)
    attn_out = None
    for h in range(key_heads):
        attn_out = attend(
            places,
            prefix_len,
            queries.reshape(SPAN, local_heads * HEAD_SIZE),
            new_keys.reshape(SPAN, key_heads * HEAD_SIZE),
            fresh_value_rows.reshape(SPAN, key_heads * HEAD_SIZE),
            arrived[h],
            h,
            key_heads,
            attn_out,
            scale,
        )
    return (attn_out, fresh_page_store)


def solution(mesh):
    return jax.shard_map(
        shards,
        mesh=mesh,
        in_specs=(
            P("dp", "tensor"),
            P(),
            P(None, "tensor"),
            P(None, "tensor"),
            P(None, "tensor"),
            P(),
            P(),
            P(("dp", "tensor"), None, None, None, None),
            P(),
            P(),
            P("dp"),
            P("dp", None, None),
        ),
        out_specs=(P("dp", "tensor"), P("dp", "tensor", None, None, None)),
        check_vma=False,
    )
```

```python
import functools
import math

import jax
import jax.numpy as jnp
from jax import lax
from jax.experimental import pallas as pl
from jax.experimental.pallas import tpu as pltpu
from jax.sharding import PartitionSpec as P

HEAD_SIZE = 128
PAGE_TOKENS = 16
SPAN = 256
NCAP = 2
MOST_PAGES = 256


EPS = 1e-06
THETA = 1000000.0
NEG = -1e30


def rms_rows(values, gain):
    mean_square = jnp.mean(values * values, axis=-1, keepdims=True)
    return values * lax.rsqrt(mean_square + EPS) * gain


def rotate(values, positions):
    half_width = values.shape[-1] // 2
    exponent = jnp.arange(half_width, dtype=jnp.float32) * (-2.0 / values.shape[-1])
    freqs = jnp.power(jnp.float32(THETA), exponent)
    angles = positions.astype(jnp.float32)[:, None] * freqs[None, :]
    cosine = jnp.cos(angles)[:, None, :]
    sine = jnp.sin(angles)[:, None, :]
    first_half = values[..., :half_width]
    second_half = values[..., half_width:]
    return jnp.concatenate(
        [first_half * cosine - second_half * sine, second_half * cosine + first_half * sine],
        axis=-1,
    )


def collect(matches, payload, capacity):
    ranks = jnp.cumsum(matches.astype(jnp.int32), axis=1) - 1
    places = jnp.arange(capacity, dtype=jnp.int32)
    landed = matches[:, :, None] & (ranks[:, :, None] == places[None, None, :])
    picked = jnp.sum(jnp.where(landed, payload[:, :, None], 0), axis=1)
    return (picked, jnp.any(landed, axis=1))


def gather_kernel(key_heads, groups, capacity, early, picked_ref, pool_ref, first_ref, second_ref):
    row = pl.program_id(0)
    last = key_heads - 1

    def pick(c, target, at):
        slot = picked_ref[row * capacity + c]
        for t in range(groups):
            target[0, t, at] = pool_ref[slot, t * key_heads + last]

    def whole(c, carry):
        slot = picked_ref[row * capacity + c]
        for h in range(last):
            for t in range(groups):
                first_ref[0, t, h * capacity + c] = pool_ref[slot, t * key_heads + h]
        return carry

    lax.fori_loop(0, capacity, whole, 0)
    for c in range(early):
        pick(c, first_ref, last * capacity + c)
    for c in range(early, capacity):
        pick(c, second_ref, c - early)


def gather_pages(picked, pool, key_heads, early):
    rows, capacity = picked.shape
    groups = pool.shape[1] // key_heads
    page = pool.shape[2:]
    units = ((key_heads - 1) * capacity + early, capacity - early)
    block = lambda n: pl.BlockSpec((1, groups, n) + page, lambda r: (r, 0, 0, 0, 0, 0))
    return pl.pallas_call(
        functools.partial(gather_kernel, key_heads, groups, capacity, early),
        grid=(rows,),
        out_shape=[jax.ShapeDtypeStruct((rows, groups, n) + page, pool.dtype) for n in units],
        in_specs=[
            pl.BlockSpec(memory_space=pltpu.SMEM),
            pl.BlockSpec(memory_space=pltpu.VMEM),
        ],
        out_specs=[block(n) for n in units],
        compiler_params=pltpu.CompilerParams(vmem_limit_bytes=32 * 2**20),
        cost_estimate=pl.CostEstimate(flops=0, bytes_accessed=4 * pool.size, transcendentals=0),
        name="gather_pages",
    )(picked.reshape(-1), pool)


BLOCK_PAGES = 64
ROW_TILES = 8


def attention_kernel(
    group, scale, base, begins, ends, places_ref, length_ref, q_ref, k_ref, v_ref, pages_ref, *refs
):
    if ends:
        out_ref, keys, values, acc, top = refs[-5:]
    else:
        acc, top, keys, values = refs[-4:]
    length = length_ref[0]
    columns = BLOCK_PAGES * PAGE_TOKENS
    live_pages = (length + PAGE_TOKENS - 1) // PAGE_TOKENS
    full = length // columns
    blocks = (length + columns - 1) // columns
    ones = jnp.ones((PAGE_TOKENS, HEAD_SIZE), jnp.bfloat16)
    factor = scale * math.log2(math.e)

    def place(i, carry):
        for u in range(8):
            j = i * 8 + u
            source = places_ref[0, j]
            at = base + places_ref[1, j]
            keys[j] = pages_ref[source, at, 0]
            values[j, :, :HEAD_SIZE] = pages_ref[source, at, 1]
            values[j, :, HEAD_SIZE:] = ones
        return carry

    lax.fori_loop(0, (live_pages + 7) // 8, place, 0)

    def spare(j, carry):
        values[j] = jnp.zeros(values.shape[1:], jnp.bfloat16)
        keys[j] = jnp.zeros(keys.shape[1:], jnp.bfloat16)
        return carry

    lax.fori_loop((live_pages + 7) // 8 * 8, blocks * BLOCK_PAGES, spare, 0)
    rows = q_ref.shape[0]
    row_ids = lax.broadcasted_iota(jnp.int32, (rows, rows), 0)
    column_ids = lax.broadcasted_iota(jnp.int32, (rows, rows), 1)
    causal = row_ids >= column_ids
    span_keys = k_ref[...]
    span_values = jnp.concatenate(
        [v_ref[...], jnp.ones((rows, HEAD_SIZE), jnp.bfloat16)], axis=1
    )
    contract_last = (((1,), (1,)), ((), ()))

    def scores_of(query, key_rows):
        return (
            lax.dot_general(query, key_rows, contract_last, preferred_element_type=jnp.float32)
            * factor
        )

    if not begins:
        acc[...] = refs[0][...]
        top[...] = refs[1][...]

    for g in range(0, group, ROW_TILES):
        queries = [q_ref[:, (g + t) * HEAD_SIZE : (g + t + 1) * HEAD_SIZE] for t in range(ROW_TILES)]
        for t in range(ROW_TILES if begins else 0):
            recent = jnp.where(causal, scores_of(queries[t], span_keys), NEG)
            peak = jnp.max(recent, axis=1, keepdims=True)
            weights = jnp.exp2(recent - peak).astype(jnp.bfloat16)
            top[g + t] = jnp.broadcast_to(peak, (rows, HEAD_SIZE))
            acc[g + t] = jnp.dot(weights, span_values, preferred_element_type=jnp.float32)

        def step(i, masked):
            start = pl.multiple_of(i * BLOCK_PAGES, BLOCK_PAGES)
            key_rows = keys[pl.ds(start, BLOCK_PAGES)].reshape(columns, HEAD_SIZE)
            value_rows = values[pl.ds(start, BLOCK_PAGES)].reshape(columns, 2 * HEAD_SIZE)
            for t in range(ROW_TILES):
                scores = scores_of(queries[t], key_rows)
                if masked:
                    positions = i * columns + lax.broadcasted_iota(jnp.int32, scores.shape, 1)
                    scores = jnp.where(positions < length, scores, NEG)
                before = top[g + t][:, :1]
                peak = jnp.maximum(before, jnp.max(scores, axis=1, keepdims=True))
                weights = jnp.exp2(scores - peak).astype(jnp.bfloat16)
                acc[g + t] = acc[g + t] * jnp.exp2(before - peak) + jnp.dot(
                    weights, value_rows, preferred_element_type=jnp.float32
                )
                top[g + t] = jnp.broadcast_to(peak, (rows, HEAD_SIZE))

        lax.fori_loop(0, full, lambda i, c: (step(i, False), c)[1], 0)

        @pl.when(full < blocks)
        def _():
            step(full, True)

        for t in range(ROW_TILES if ends else 0):
            mixed = acc[g + t]
            out_ref[:, (g + t) * HEAD_SIZE : (g + t + 1) * HEAD_SIZE] = (
                mixed[:, :HEAD_SIZE] / mixed[:, HEAD_SIZE:]
            ).astype(jnp.bfloat16)


def attend(
    places, length, queries, new_keys, new_values, pages, h, key_heads, scale, base, state, out, ends
):
    rows, width = queries.shape
    part = width // key_heads
    group = part // HEAD_SIZE
    most = places.shape[1]
    in_specs = [
        pl.BlockSpec(memory_space=pltpu.SMEM),
        pl.BlockSpec(memory_space=pltpu.SMEM),
        pl.BlockSpec((rows, part), lambda i: (0, h)),
        pl.BlockSpec((rows, HEAD_SIZE), lambda i: (0, h)),
        pl.BlockSpec((rows, HEAD_SIZE), lambda i: (0, h)),
        pl.BlockSpec(pages.shape, lambda i: (0,) * pages.ndim),
    ]
    operands = [places, length, queries, new_keys, new_values, pages]
    state_shapes = [(group, rows, 2 * HEAD_SIZE), (group, rows, HEAD_SIZE)]
    state_specs = [pl.BlockSpec(shape, lambda i: (0, 0, 0)) for shape in state_shapes]
    if state is not None:
        in_specs += state_specs
        operands += state
    aliases = {}
    if ends and out is not None:
        in_specs.append(pl.BlockSpec(memory_space=pl.ANY))
        operands.append(out)
        aliases = {len(operands) - 1: 0}
    scratch = [
        pltpu.VMEM((most, PAGE_TOKENS, HEAD_SIZE), jnp.bfloat16),
        pltpu.VMEM((most, PAGE_TOKENS, 2 * HEAD_SIZE), jnp.bfloat16),
    ]
    if ends:
        out_shape = jax.ShapeDtypeStruct((rows, width), jnp.bfloat16)
        out_specs = pl.BlockSpec((rows, part), lambda i: (0, h))
        scratch += [pltpu.VMEM(shape, jnp.float32) for shape in state_shapes]
    else:
        out_shape = [jax.ShapeDtypeStruct(shape, jnp.float32) for shape in state_shapes]
        out_specs = state_specs
    return pl.pallas_call(
        functools.partial(attention_kernel, group, scale, base, state is None, ends),
        grid=(1,),
        out_shape=out_shape,
        in_specs=in_specs,
        out_specs=out_specs,
        scratch_shapes=scratch,
        input_output_aliases=aliases,
        compiler_params=pltpu.CompilerParams(vmem_limit_bytes=44 * 2**20),
        cost_estimate=pl.CostEstimate(
            flops=4 * rows * part * most * PAGE_TOKENS,
            bytes_accessed=2 * pages.size,
            transcendentals=rows * group * most * PAGE_TOKENS,
        ),
        name="attend_head",
    )(*operands)


def shards(
    hidden,
    norm_gain,
    w_query,
    key_projection_weight,
    value_projection_weight,
    query_gain,
    key_gain,
    kv_pool,
    page_owner,
    page_slot,
    prefix_len,
    new_owner,
):
    data_ways = lax.axis_size("dp")
    tensor_ways = lax.axis_size("tensor")
    request = lax.axis_index("dp")
    slot_count = kv_pool.shape[0]
    capacity = slot_count // data_ways
    key_heads = key_projection_weight.shape[1] // HEAD_SIZE
    local_heads = w_query.shape[1] // HEAD_SIZE
    scale = 1.0 / math.sqrt(HEAD_SIZE)
    own_row = lax.dynamic_index_in_dim(page_owner, request, 0, keepdims=False)
    my_device = request * tensor_ways + lax.axis_index("tensor")
    picked, unused = collect(page_owner == my_device, page_slot, capacity)
    early = max(1, capacity // 2)
    outgoing = gather_pages(picked, kv_pool, key_heads, early)
    sources = data_ways * tensor_ways

    def exchange(pages):
        return lax.all_to_all(
            pages.reshape((sources,) + pages.shape[2:]),
            ("dp", "tensor"),
            split_axis=0,
            concat_axis=0,
            tiled=True,
        )

    first_pages = exchange(outgoing[0])
    full_rows = lax.all_gather(hidden, "tensor", axis=1, tiled=True)
    full_rows, outgoing = lax.optimization_barrier((full_rows, outgoing))
    normalized_rows = rms_rows(full_rows.astype(jnp.float32), norm_gain).astype(jnp.bfloat16)
    length = prefix_len[0]
    offsets = jnp.arange(SPAN, dtype=jnp.int32)
    positions = length + offsets
    query_flat = jnp.dot(normalized_rows, w_query, preferred_element_type=jnp.float32).reshape(
        SPAN, local_heads, HEAD_SIZE
    )
    flattened_keys = jnp.dot(
        normalized_rows, key_projection_weight, preferred_element_type=jnp.float32
    ).reshape(SPAN, key_heads, HEAD_SIZE)
    queries = rotate(rms_rows(query_flat, query_gain), positions).astype(jnp.bfloat16)
    queries, first_pages, late = lax.optimization_barrier((queries, first_pages, outgoing[1]))
    second_pages = exchange(late)
    new_keys = rotate(rms_rows(flattened_keys, key_gain), positions).astype(jnp.bfloat16)
    fresh_value_rows = (
        jnp.dot(normalized_rows, value_projection_weight, preferred_element_type=jnp.float32)
        .astype(jnp.bfloat16)
        .reshape(SPAN, key_heads, HEAD_SIZE)
    )
    page_count = SPAN // PAGE_TOKENS
    stacked_pages = jnp.stack([new_keys, fresh_value_rows], axis=2)
    fresh_pages = (
        stacked_pages.reshape(page_count, PAGE_TOKENS, key_heads, 2, HEAD_SIZE)
        .transpose(0, 2, 3, 1, 4)
        .reshape(page_count, key_heads * 2 * PAGE_TOKENS * HEAD_SIZE)
    )
    targets = new_owner[0, :, 0]
    page_index = jnp.arange(page_count, dtype=jnp.int32)
    earlier = page_index[None, :] < page_index[:, None]
    ranks = jnp.sum((targets[:, None] == targets[None, :]) & earlier, axis=1)
    slot_index = jnp.arange(data_ways * NCAP, dtype=jnp.int32)
    selector = ((targets * NCAP + ranks)[None, :] == slot_index[:, None]).astype(jnp.bfloat16)
    outgoing_pages = jnp.dot(selector, fresh_pages, preferred_element_type=jnp.float32).astype(
        jnp.bfloat16
    )
    outgoing_pages = outgoing_pages.reshape(data_ways * NCAP, key_heads, 2, PAGE_TOKENS, HEAD_SIZE)
    outgoing_pages = outgoing_pages.reshape(
        (data_ways, NCAP) + outgoing_pages.shape[1:]
    )
    every = lax.all_gather(outgoing_pages, "dp", axis=0)
    same = own_row[:, None] == own_row[None, :]
    later = jnp.arange(MOST_PAGES)[:, None] > jnp.arange(MOST_PAGES)[None, :]
    page_ranks = jnp.sum(same & later, axis=1).astype(jnp.int32)
    live_tokens = jnp.clip(
        length - jnp.arange(MOST_PAGES, dtype=jnp.int32) * PAGE_TOKENS, 0, PAGE_TOKENS
    )
    everywhere = jnp.stack([own_row, page_ranks])

    def subset(chosen, shift):
        order = jnp.cumsum(chosen.astype(jnp.int32)) - 1
        landed = chosen[:, None] & (order[:, None] == jnp.arange(MOST_PAGES)[None, :])
        table = jnp.stack([own_row, page_ranks - shift])
        table = jnp.sum(jnp.where(landed[None], table[:, :, None], 0), axis=1)
        return (table, jnp.sum(jnp.where(chosen, live_tokens, 0)).reshape(1))

    first_table, first_length = subset(page_ranks < early, 0)
    second_table, second_length = subset(page_ranks >= early, early)
    tensors = (
        queries.reshape(SPAN, local_heads * HEAD_SIZE),
        new_keys.reshape(SPAN, key_heads * HEAD_SIZE),
        fresh_value_rows.reshape(SPAN, key_heads * HEAD_SIZE),
    )
    attn_out = None
    last = key_heads - 1
    for h in range(last):
        attn_out = attend(
            everywhere, prefix_len, *tensors, first_pages, h, key_heads, scale, h * capacity, None, attn_out, True
        )
    state = attend(
        first_table, first_length, *tensors, first_pages, last, key_heads, scale, last * capacity, None, None, False
    )
    every, state = lax.optimization_barrier((every, state))
    fresh_page_store = lax.dynamic_index_in_dim(every, request, 1, keepdims=False)
    fresh_page_store = fresh_page_store.reshape((data_ways * NCAP,) + outgoing_pages.shape[2:])
    attn_out = attend(
        second_table, second_length, *tensors, second_pages, last, key_heads, scale, 0, list(state), attn_out, True
    )
    return (attn_out, fresh_page_store)


def solution(mesh):
    return jax.shard_map(
        shards,
        mesh=mesh,
        in_specs=(
            P("dp", "tensor"),
            P(),
            P(None, "tensor"),
            P(None, "tensor"),
            P(None, "tensor"),
            P(),
            P(),
            P(("dp", "tensor"), None, None, None, None),
            P(),
            P(),
            P("dp"),
            P("dp", None, None),
        ),
        out_specs=(P("dp", "tensor"), P("dp", "tensor", None, None, None)),
        check_vma=False,
    )
```

```python
import functools
import math

import jax
import jax.numpy as jnp
from jax import lax
from jax.experimental import pallas as pl
from jax.experimental.pallas import tpu as pltpu
from jax.sharding import PartitionSpec as P

HEAD_SIZE = 128
PAGE_TOKENS = 16
SPAN = 256
NCAP = 2
MOST_PAGES = 256


EPS = 1e-06
THETA = 1000000.0
NEG = -1e30


def rms_rows(values, gain):
    mean_square = jnp.mean(values * values, axis=-1, keepdims=True)
    return values * lax.rsqrt(mean_square + EPS) * gain


def rotate(values, positions):
    half_width = values.shape[-1] // 2
    exponent = jnp.arange(half_width, dtype=jnp.float32) * (-2.0 / values.shape[-1])
    freqs = jnp.power(jnp.float32(THETA), exponent)
    angles = positions.astype(jnp.float32)[:, None] * freqs[None, :]
    cosine = jnp.cos(angles)[:, None, :]
    sine = jnp.sin(angles)[:, None, :]
    first_half = values[..., :half_width]
    second_half = values[..., half_width:]
    return jnp.concatenate(
        [first_half * cosine - second_half * sine, second_half * cosine + first_half * sine],
        axis=-1,
    )


def collect(matches, payload, capacity):
    ranks = jnp.cumsum(matches.astype(jnp.int32), axis=1) - 1
    places = jnp.arange(capacity, dtype=jnp.int32)
    landed = matches[:, :, None] & (ranks[:, :, None] == places[None, None, :])
    picked = jnp.sum(jnp.where(landed, payload[:, :, None], 0), axis=1)
    return (picked, jnp.any(landed, axis=1))


def gather_kernel(key_heads, groups, capacity, early, picked_ref, pool_ref, first_ref, second_ref):
    row = pl.program_id(0)
    last = key_heads - 1

    def pick(c, target, at):
        slot = picked_ref[row * capacity + c]
        for t in range(groups):
            target[0, t, at] = pool_ref[slot, t * key_heads + last]

    def whole(c, carry):
        slot = picked_ref[row * capacity + c]
        for h in range(last):
            for t in range(groups):
                first_ref[0, t, h * capacity + c] = pool_ref[slot, t * key_heads + h]
        return carry

    lax.fori_loop(0, capacity, whole, 0)
    for c in range(early):
        pick(c, first_ref, last * capacity + c)
    for c in range(early, capacity):
        pick(c, second_ref, c - early)


def gather_pages(picked, pool, key_heads, early):
    rows, capacity = picked.shape
    groups = pool.shape[1] // key_heads
    page = pool.shape[2:]
    units = ((key_heads - 1) * capacity + early, capacity - early)
    block = lambda n: pl.BlockSpec((1, groups, n) + page, lambda r: (r, 0, 0, 0, 0, 0))
    return pl.pallas_call(
        functools.partial(gather_kernel, key_heads, groups, capacity, early),
        grid=(rows,),
        out_shape=[jax.ShapeDtypeStruct((rows, groups, n) + page, pool.dtype) for n in units],
        in_specs=[
            pl.BlockSpec(memory_space=pltpu.SMEM),
            pl.BlockSpec(memory_space=pltpu.VMEM),
        ],
        out_specs=[block(n) for n in units],
        compiler_params=pltpu.CompilerParams(vmem_limit_bytes=60 * 2**20),
        cost_estimate=pl.CostEstimate(flops=0, bytes_accessed=4 * pool.size, transcendentals=0),
        name="gather_pages",
    )(picked.reshape(-1), pool)


BLOCK_PAGES = 64
ROW_TILES = 8


def attention_kernel(
    group, scale, base, begins, ends, places_ref, length_ref, q_ref, k_ref, v_ref, pages_ref, *refs
):
    if ends:
        out_ref, keys, values, acc, top = refs[-5:]
    else:
        acc, top, keys, values = refs[-4:]
    length = length_ref[0]
    columns = BLOCK_PAGES * PAGE_TOKENS
    live_pages = (length + PAGE_TOKENS - 1) // PAGE_TOKENS
    full = length // columns
    blocks = (length + columns - 1) // columns
    ones = jnp.ones((PAGE_TOKENS, HEAD_SIZE), jnp.bfloat16)
    factor = scale * math.log2(math.e)

    def place(i, carry):
        for u in range(8):
            j = i * 8 + u
            source = places_ref[0, j]
            at = base + places_ref[1, j]
            keys[j] = pages_ref[source, at, 0]
            values[j, :, :HEAD_SIZE] = pages_ref[source, at, 1]
            values[j, :, HEAD_SIZE:] = ones
        return carry

    lax.fori_loop(0, (live_pages + 7) // 8, place, 0)

    def spare(j, carry):
        values[j] = jnp.zeros(values.shape[1:], jnp.bfloat16)
        keys[j] = jnp.zeros(keys.shape[1:], jnp.bfloat16)
        return carry

    lax.fori_loop((live_pages + 7) // 8 * 8, blocks * BLOCK_PAGES, spare, 0)
    rows = q_ref.shape[0]
    row_ids = lax.broadcasted_iota(jnp.int32, (rows, rows), 0)
    column_ids = lax.broadcasted_iota(jnp.int32, (rows, rows), 1)
    causal = row_ids >= column_ids
    span_keys = k_ref[...]
    span_values = jnp.concatenate(
        [v_ref[...], jnp.ones((rows, HEAD_SIZE), jnp.bfloat16)], axis=1
    )
    contract_last = (((1,), (1,)), ((), ()))

    def scores_of(query, key_rows):
        return (
            lax.dot_general(query, key_rows, contract_last, preferred_element_type=jnp.float32)
            * factor
        )

    if not begins:
        acc[...] = refs[0][...]
        top[...] = refs[1][...]

    for g in range(0, group, ROW_TILES):
        queries = [q_ref[:, (g + t) * HEAD_SIZE : (g + t + 1) * HEAD_SIZE] for t in range(ROW_TILES)]
        for t in range(ROW_TILES if begins else 0):
            recent = jnp.where(causal, scores_of(queries[t], span_keys), NEG)
            peak = jnp.max(recent, axis=1, keepdims=True)
            weights = jnp.exp2(recent - peak).astype(jnp.bfloat16)
            top[g + t] = jnp.broadcast_to(peak, (rows, HEAD_SIZE))
            acc[g + t] = jnp.dot(weights, span_values, preferred_element_type=jnp.float32)

        def step(i, masked):
            start = pl.multiple_of(i * BLOCK_PAGES, BLOCK_PAGES)
            key_rows = keys[pl.ds(start, BLOCK_PAGES)].reshape(columns, HEAD_SIZE)
            value_rows = values[pl.ds(start, BLOCK_PAGES)].reshape(columns, 2 * HEAD_SIZE)
            for t in range(ROW_TILES):
                scores = scores_of(queries[t], key_rows)
                if masked:
                    positions = i * columns + lax.broadcasted_iota(jnp.int32, scores.shape, 1)
                    scores = jnp.where(positions < length, scores, NEG)
                before = top[g + t][:, :1]
                peak = jnp.maximum(before, jnp.max(scores, axis=1, keepdims=True))
                weights = jnp.exp2(scores - peak).astype(jnp.bfloat16)
                acc[g + t] = acc[g + t] * jnp.exp2(before - peak) + jnp.dot(
                    weights, value_rows, preferred_element_type=jnp.float32
                )
                top[g + t] = jnp.broadcast_to(peak, (rows, HEAD_SIZE))

        lax.fori_loop(0, full, lambda i, c: (step(i, False), c)[1], 0)

        @pl.when(full < blocks)
        def _():
            step(full, True)

        for t in range(ROW_TILES if ends else 0):
            mixed = acc[g + t]
            out_ref[:, (g + t) * HEAD_SIZE : (g + t + 1) * HEAD_SIZE] = (
                mixed[:, :HEAD_SIZE] / mixed[:, HEAD_SIZE:]
            ).astype(jnp.bfloat16)


def attend(
    places, length, queries, new_keys, new_values, pages, h, key_heads, scale, base, state, out, ends
):
    rows, width = queries.shape
    part = width // key_heads
    group = part // HEAD_SIZE
    most = places.shape[1]
    in_specs = [
        pl.BlockSpec(memory_space=pltpu.SMEM),
        pl.BlockSpec(memory_space=pltpu.SMEM),
        pl.BlockSpec((rows, part), lambda i: (0, h)),
        pl.BlockSpec((rows, HEAD_SIZE), lambda i: (0, h)),
        pl.BlockSpec((rows, HEAD_SIZE), lambda i: (0, h)),
        pl.BlockSpec(pages.shape, lambda i: (0,) * pages.ndim),
    ]
    operands = [places, length, queries, new_keys, new_values, pages]
    state_shapes = [(group, rows, 2 * HEAD_SIZE), (group, rows, HEAD_SIZE)]
    state_specs = [pl.BlockSpec(shape, lambda i: (0, 0, 0)) for shape in state_shapes]
    if state is not None:
        in_specs += state_specs
        operands += state
    aliases = {}
    if ends and out is not None:
        in_specs.append(pl.BlockSpec(memory_space=pl.ANY))
        operands.append(out)
        aliases = {len(operands) - 1: 0}
    scratch = [
        pltpu.VMEM((most, PAGE_TOKENS, HEAD_SIZE), jnp.bfloat16),
        pltpu.VMEM((most, PAGE_TOKENS, 2 * HEAD_SIZE), jnp.bfloat16),
    ]
    if ends:
        out_shape = jax.ShapeDtypeStruct((rows, width), jnp.bfloat16)
        out_specs = pl.BlockSpec((rows, part), lambda i: (0, h))
        scratch += [pltpu.VMEM(shape, jnp.float32) for shape in state_shapes]
    else:
        out_shape = [jax.ShapeDtypeStruct(shape, jnp.float32) for shape in state_shapes]
        out_specs = state_specs
    return pl.pallas_call(
        functools.partial(attention_kernel, group, scale, base, state is None, ends),
        grid=(1,),
        out_shape=out_shape,
        in_specs=in_specs,
        out_specs=out_specs,
        scratch_shapes=scratch,
        input_output_aliases=aliases,
        compiler_params=pltpu.CompilerParams(vmem_limit_bytes=60 * 2**20),
        cost_estimate=pl.CostEstimate(
            flops=4 * rows * part * most * PAGE_TOKENS,
            bytes_accessed=2 * pages.size,
            transcendentals=rows * group * most * PAGE_TOKENS,
        ),
        name="attend_head",
    )(*operands)


def shards(
    hidden,
    norm_gain,
    w_query,
    key_projection_weight,
    value_projection_weight,
    query_gain,
    key_gain,
    kv_pool,
    page_owner,
    page_slot,
    prefix_len,
    new_owner,
):
    data_ways = lax.axis_size("dp")
    tensor_ways = lax.axis_size("tensor")
    request = lax.axis_index("dp")
    slot_count = kv_pool.shape[0]
    capacity = slot_count // data_ways
    key_heads = key_projection_weight.shape[1] // HEAD_SIZE
    local_heads = w_query.shape[1] // HEAD_SIZE
    scale = 1.0 / math.sqrt(HEAD_SIZE)
    own_row = lax.dynamic_index_in_dim(page_owner, request, 0, keepdims=False)
    my_device = request * tensor_ways + lax.axis_index("tensor")
    picked, unused = collect(page_owner == my_device, page_slot, capacity)
    early = max(1, capacity // 2)
    outgoing = gather_pages(picked, kv_pool, key_heads, early)
    sources = data_ways * tensor_ways

    def exchange(pages):
        return lax.all_to_all(
            pages.reshape((sources,) + pages.shape[2:]),
            ("dp", "tensor"),
            split_axis=0,
            concat_axis=0,
            tiled=True,
        )

    first_pages = exchange(outgoing[0])
    full_rows = lax.all_gather(hidden, "tensor", axis=1, tiled=True)
    full_rows, outgoing = lax.optimization_barrier((full_rows, outgoing))
    normalized_rows = rms_rows(full_rows.astype(jnp.float32), norm_gain).astype(jnp.bfloat16)
    length = prefix_len[0]
    offsets = jnp.arange(SPAN, dtype=jnp.int32)
    positions = length + offsets
    query_flat = jnp.dot(normalized_rows, w_query, preferred_element_type=jnp.float32).reshape(
        SPAN, local_heads, HEAD_SIZE
    )
    flattened_keys = jnp.dot(
        normalized_rows, key_projection_weight, preferred_element_type=jnp.float32
    ).reshape(SPAN, key_heads, HEAD_SIZE)
    queries = rotate(rms_rows(query_flat, query_gain), positions).astype(jnp.bfloat16)
    queries, first_pages, late = lax.optimization_barrier((queries, first_pages, outgoing[1]))
    second_pages = exchange(late)
    new_keys = rotate(rms_rows(flattened_keys, key_gain), positions).astype(jnp.bfloat16)
    fresh_value_rows = (
        jnp.dot(normalized_rows, value_projection_weight, preferred_element_type=jnp.float32)
        .astype(jnp.bfloat16)
        .reshape(SPAN, key_heads, HEAD_SIZE)
    )
    page_count = SPAN // PAGE_TOKENS
    stacked_pages = jnp.stack([new_keys, fresh_value_rows], axis=2)
    fresh_pages = (
        stacked_pages.reshape(page_count, PAGE_TOKENS, key_heads, 2, HEAD_SIZE)
        .transpose(0, 2, 3, 1, 4)
        .reshape(page_count, key_heads * 2 * PAGE_TOKENS * HEAD_SIZE)
    )
    targets = new_owner[0, :, 0]
    page_index = jnp.arange(page_count, dtype=jnp.int32)
    earlier = page_index[None, :] < page_index[:, None]
    ranks = jnp.sum((targets[:, None] == targets[None, :]) & earlier, axis=1)
    slot_index = jnp.arange(data_ways * NCAP, dtype=jnp.int32)
    selector = ((targets * NCAP + ranks)[None, :] == slot_index[:, None]).astype(jnp.bfloat16)
    outgoing_pages = jnp.dot(selector, fresh_pages, preferred_element_type=jnp.float32).astype(
        jnp.bfloat16
    )
    outgoing_pages = outgoing_pages.reshape(data_ways * NCAP, key_heads, 2, PAGE_TOKENS, HEAD_SIZE)
    outgoing_pages = outgoing_pages.reshape(
        (data_ways, NCAP) + outgoing_pages.shape[1:]
    )
    every = lax.all_gather(outgoing_pages, "dp", axis=0)
    same = own_row[:, None] == own_row[None, :]
    later = jnp.arange(MOST_PAGES)[:, None] > jnp.arange(MOST_PAGES)[None, :]
    page_ranks = jnp.sum(same & later, axis=1).astype(jnp.int32)
    live_tokens = jnp.clip(
        length - jnp.arange(MOST_PAGES, dtype=jnp.int32) * PAGE_TOKENS, 0, PAGE_TOKENS
    )
    everywhere = jnp.stack([own_row, page_ranks])

    def subset(chosen, shift):
        order = jnp.cumsum(chosen.astype(jnp.int32)) - 1
        landed = chosen[:, None] & (order[:, None] == jnp.arange(MOST_PAGES)[None, :])
        table = jnp.stack([own_row, page_ranks - shift])
        table = jnp.sum(jnp.where(landed[None], table[:, :, None], 0), axis=1)
        return (table, jnp.sum(jnp.where(chosen, live_tokens, 0)).reshape(1))

    first_table, first_length = subset(page_ranks < early, 0)
    second_table, second_length = subset(page_ranks >= early, early)
    tensors = (
        queries.reshape(SPAN, local_heads * HEAD_SIZE),
        new_keys.reshape(SPAN, key_heads * HEAD_SIZE),
        fresh_value_rows.reshape(SPAN, key_heads * HEAD_SIZE),
    )
    attn_out = None
    last = key_heads - 1
    for h in range(last):
        attn_out = attend(
            everywhere, prefix_len, *tensors, first_pages, h, key_heads, scale, h * capacity, None, attn_out, True
        )
    if attn_out is not None:
        attn_out, first_length = lax.optimization_barrier((attn_out, first_length))
    state = attend(
        first_table, first_length, *tensors, first_pages, last, key_heads, scale, last * capacity, None, None, False
    )
    every, state = lax.optimization_barrier((every, state))
    fresh_page_store = lax.dynamic_index_in_dim(every, request, 1, keepdims=False)
    fresh_page_store = fresh_page_store.reshape((data_ways * NCAP,) + outgoing_pages.shape[2:])
    attn_out = attend(
        second_table, second_length, *tensors, second_pages, last, key_heads, scale, 0, list(state), attn_out, True
    )
    return (attn_out, fresh_page_store)


def solution(mesh):
    return jax.shard_map(
        shards,
        mesh=mesh,
        in_specs=(
            P("dp", "tensor"),
            P(),
            P(None, "tensor"),
            P(None, "tensor"),
            P(None, "tensor"),
            P(),
            P(),
            P(("dp", "tensor"), None, None, None, None),
            P(),
            P(),
            P("dp"),
            P("dp", None, None),
        ),
        out_specs=(P("dp", "tensor"), P("dp", "tensor", None, None, None)),
        check_vma=False,
    )
```

```python
import functools
import math

import jax
import jax.numpy as jnp
from jax import lax
from jax.experimental import pallas as pl
from jax.experimental.pallas import tpu as pltpu
from jax.sharding import PartitionSpec as P

HEAD_SIZE = 128
PAGE_TOKENS = 16
SPAN = 256
NCAP = 2
MOST_PAGES = 256


EPS = 1e-06
THETA = 1000000.0
NEG = -1e30


def rms_rows(values, gain):
    mean_square = jnp.mean(values * values, axis=-1, keepdims=True)
    return values * lax.rsqrt(mean_square + EPS) * gain


def rotate(values, positions):
    half_width = values.shape[-1] // 2
    exponent = jnp.arange(half_width, dtype=jnp.float32) * (-2.0 / values.shape[-1])
    freqs = jnp.power(jnp.float32(THETA), exponent)
    angles = positions.astype(jnp.float32)[:, None] * freqs[None, :]
    cosine = jnp.cos(angles)[:, None, :]
    sine = jnp.sin(angles)[:, None, :]
    first_half = values[..., :half_width]
    second_half = values[..., half_width:]
    return jnp.concatenate(
        [first_half * cosine - second_half * sine, second_half * cosine + first_half * sine],
        axis=-1,
    )


def collect(matches, payload, capacity):
    ranks = jnp.cumsum(matches.astype(jnp.int32), axis=1) - 1
    places = jnp.arange(capacity, dtype=jnp.int32)
    landed = matches[:, :, None] & (ranks[:, :, None] == places[None, None, :])
    picked = jnp.sum(jnp.where(landed, payload[:, :, None], 0), axis=1)
    return (picked, jnp.any(landed, axis=1))


def gather_kernel(key_heads, groups, capacity, early, picked_ref, pool_ref, first_ref, second_ref):
    row = pl.program_id(0)
    last = key_heads - 1

    def pick(c, target, at):
        slot = picked_ref[row * capacity + c]
        for t in range(groups):
            target[0, t, at] = pool_ref[slot, t * key_heads + last]

    def whole(c, carry):
        slot = picked_ref[row * capacity + c]
        for h in range(last):
            for t in range(groups):
                first_ref[0, t, h * capacity + c] = pool_ref[slot, t * key_heads + h]
        return carry

    lax.fori_loop(0, capacity, whole, 0)
    for c in range(early):
        pick(c, first_ref, last * capacity + c)
    for c in range(early, capacity):
        pick(c, second_ref, c - early)


def gather_pages(picked, pool, key_heads, early):
    rows, capacity = picked.shape
    groups = pool.shape[1] // key_heads
    page = pool.shape[2:]
    units = ((key_heads - 1) * capacity + early, capacity - early)
    block = lambda n: pl.BlockSpec((1, groups, n) + page, lambda r: (r, 0, 0, 0, 0, 0))
    return pl.pallas_call(
        functools.partial(gather_kernel, key_heads, groups, capacity, early),
        grid=(rows,),
        out_shape=[jax.ShapeDtypeStruct((rows, groups, n) + page, pool.dtype) for n in units],
        in_specs=[
            pl.BlockSpec(memory_space=pltpu.SMEM),
            pl.BlockSpec(memory_space=pltpu.VMEM),
        ],
        out_specs=[block(n) for n in units],
        compiler_params=pltpu.CompilerParams(vmem_limit_bytes=60 * 2**20),
        cost_estimate=pl.CostEstimate(flops=0, bytes_accessed=4 * pool.size, transcendentals=0),
        name="gather_pages",
    )(picked.reshape(-1), pool)


BLOCK_PAGES = 64
ROW_TILES = 8


def attention_kernel(
    group, scale, base, begins, ends, places_ref, length_ref, q_ref, k_ref, v_ref, pages_ref, *refs
):
    if ends:
        out_ref, keys, values, acc, top = refs[-5:]
    else:
        acc, top, keys, values = refs[-4:]
    length = length_ref[0]
    columns = BLOCK_PAGES * PAGE_TOKENS
    live_pages = (length + PAGE_TOKENS - 1) // PAGE_TOKENS
    full = length // columns
    blocks = (length + columns - 1) // columns
    ones = jnp.ones((PAGE_TOKENS, HEAD_SIZE), jnp.bfloat16)
    factor = scale * math.log2(math.e)

    def place(i, carry):
        for u in range(8):
            j = i * 8 + u
            source = places_ref[0, j]
            at = base + places_ref[1, j]
            keys[j] = pages_ref[source, at, 0]
            values[j, :, :HEAD_SIZE] = pages_ref[source, at, 1]
            values[j, :, HEAD_SIZE:] = ones
        return carry

    lax.fori_loop(0, (live_pages + 7) // 8, place, 0)

    def spare(j, carry):
        values[j] = jnp.zeros(values.shape[1:], jnp.bfloat16)
        keys[j] = jnp.zeros(keys.shape[1:], jnp.bfloat16)
        return carry

    lax.fori_loop((live_pages + 7) // 8 * 8, blocks * BLOCK_PAGES, spare, 0)
    rows = q_ref.shape[0]
    row_ids = lax.broadcasted_iota(jnp.int32, (rows, rows), 0)
    column_ids = lax.broadcasted_iota(jnp.int32, (rows, rows), 1)
    causal = row_ids >= column_ids
    span_keys = k_ref[...]
    span_values = jnp.concatenate(
        [v_ref[...], jnp.ones((rows, HEAD_SIZE), jnp.bfloat16)], axis=1
    )
    contract_last = (((1,), (1,)), ((), ()))

    def scores_of(query, key_rows):
        return (
            lax.dot_general(query, key_rows, contract_last, preferred_element_type=jnp.float32)
            * factor
        )

    if not begins:
        acc[...] = refs[0][...]
        top[...] = refs[1][...]

    for g in range(0, group, ROW_TILES):
        queries = [q_ref[:, (g + t) * HEAD_SIZE : (g + t + 1) * HEAD_SIZE] for t in range(ROW_TILES)]
        for t in range(ROW_TILES if begins else 0):
            recent = jnp.where(causal, scores_of(queries[t], span_keys), NEG)
            peak = jnp.max(recent, axis=1, keepdims=True)
            weights = jnp.exp2(recent - peak).astype(jnp.bfloat16)
            top[g + t] = jnp.broadcast_to(peak, (rows, HEAD_SIZE))
            acc[g + t] = jnp.dot(weights, span_values, preferred_element_type=jnp.float32)

        def step(i, masked):
            start = pl.multiple_of(i * BLOCK_PAGES, BLOCK_PAGES)
            key_rows = keys[pl.ds(start, BLOCK_PAGES)].reshape(columns, HEAD_SIZE)
            value_rows = values[pl.ds(start, BLOCK_PAGES)].reshape(columns, 2 * HEAD_SIZE)
            for t in range(ROW_TILES):
                scores = scores_of(queries[t], key_rows)
                if masked:
                    positions = i * columns + lax.broadcasted_iota(jnp.int32, scores.shape, 1)
                    scores = jnp.where(positions < length, scores, NEG)
                before = top[g + t][:, :1]
                peak = jnp.maximum(before, jnp.max(scores, axis=1, keepdims=True))
                weights = jnp.exp2(scores - peak).astype(jnp.bfloat16)
                acc[g + t] = acc[g + t] * jnp.exp2(before - peak) + jnp.dot(
                    weights, value_rows, preferred_element_type=jnp.float32
                )
                top[g + t] = jnp.broadcast_to(peak, (rows, HEAD_SIZE))

        lax.fori_loop(0, full, lambda i, c: (step(i, False), c)[1], 0)

        @pl.when(full < blocks)
        def _():
            step(full, True)

        for t in range(ROW_TILES if ends else 0):
            mixed = acc[g + t]
            out_ref[:, (g + t) * HEAD_SIZE : (g + t + 1) * HEAD_SIZE] = (
                mixed[:, :HEAD_SIZE] / mixed[:, HEAD_SIZE:]
            ).astype(jnp.bfloat16)


def attend(
    places, length, queries, new_keys, new_values, pages, h, key_heads, scale, base, state, out, ends
):
    rows, width = queries.shape
    part = width // key_heads
    group = part // HEAD_SIZE
    most = places.shape[1]
    in_specs = [
        pl.BlockSpec(memory_space=pltpu.SMEM),
        pl.BlockSpec(memory_space=pltpu.SMEM),
        pl.BlockSpec((rows, part), lambda i: (0, h)),
        pl.BlockSpec((rows, HEAD_SIZE), lambda i: (0, h)),
        pl.BlockSpec((rows, HEAD_SIZE), lambda i: (0, h)),
        pl.BlockSpec(pages.shape, lambda i: (0,) * pages.ndim),
    ]
    operands = [places, length, queries, new_keys, new_values, pages]
    state_shapes = [(group, rows, 2 * HEAD_SIZE), (group, rows, HEAD_SIZE)]
    state_specs = [pl.BlockSpec(shape, lambda i: (0, 0, 0)) for shape in state_shapes]
    if state is not None:
        in_specs += state_specs
        operands += state
    aliases = {}
    if ends and out is not None:
        in_specs.append(pl.BlockSpec(memory_space=pl.ANY))
        operands.append(out)
        aliases = {len(operands) - 1: 0}
    scratch = [
        pltpu.VMEM((most, PAGE_TOKENS, HEAD_SIZE), jnp.bfloat16),
        pltpu.VMEM((most, PAGE_TOKENS, 2 * HEAD_SIZE), jnp.bfloat16),
    ]
    if ends:
        out_shape = jax.ShapeDtypeStruct((rows, width), jnp.bfloat16)
        out_specs = pl.BlockSpec((rows, part), lambda i: (0, h))
        scratch += [pltpu.VMEM(shape, jnp.float32) for shape in state_shapes]
    else:
        out_shape = [jax.ShapeDtypeStruct(shape, jnp.float32) for shape in state_shapes]
        out_specs = state_specs
    return pl.pallas_call(
        functools.partial(attention_kernel, group, scale, base, state is None, ends),
        grid=(1,),
        out_shape=out_shape,
        in_specs=in_specs,
        out_specs=out_specs,
        scratch_shapes=scratch,
        input_output_aliases=aliases,
        compiler_params=pltpu.CompilerParams(vmem_limit_bytes=60 * 2**20),
        cost_estimate=pl.CostEstimate(
            flops=4 * rows * part * most * PAGE_TOKENS,
            bytes_accessed=2 * pages.size,
            transcendentals=rows * group * most * PAGE_TOKENS,
        ),
        name="attend_head",
    )(*operands)


def shards(
    hidden,
    norm_gain,
    w_query,
    key_projection_weight,
    value_projection_weight,
    query_gain,
    key_gain,
    kv_pool,
    page_owner,
    page_slot,
    prefix_len,
    new_owner,
):
    data_ways = lax.axis_size("dp")
    tensor_ways = lax.axis_size("tensor")
    request = lax.axis_index("dp")
    slot_count = kv_pool.shape[0]
    capacity = slot_count // data_ways
    key_heads = key_projection_weight.shape[1] // HEAD_SIZE
    local_heads = w_query.shape[1] // HEAD_SIZE
    scale = 1.0 / math.sqrt(HEAD_SIZE)
    own_row = lax.dynamic_index_in_dim(page_owner, request, 0, keepdims=False)
    my_device = request * tensor_ways + lax.axis_index("tensor")
    picked, unused = collect(page_owner == my_device, page_slot, capacity)
    early = max(1, capacity // 3)
    outgoing = gather_pages(picked, kv_pool, key_heads, early)
    sources = data_ways * tensor_ways

    def exchange(pages):
        return lax.all_to_all(
            pages.reshape((sources,) + pages.shape[2:]),
            ("dp", "tensor"),
            split_axis=0,
            concat_axis=0,
            tiled=True,
        )

    first_pages = exchange(outgoing[0])
    full_rows = lax.all_gather(hidden, "tensor", axis=1, tiled=True)
    full_rows, outgoing = lax.optimization_barrier((full_rows, outgoing))
    normalized_rows = rms_rows(full_rows.astype(jnp.float32), norm_gain).astype(jnp.bfloat16)
    length = prefix_len[0]
    offsets = jnp.arange(SPAN, dtype=jnp.int32)
    positions = length + offsets
    query_flat = jnp.dot(normalized_rows, w_query, preferred_element_type=jnp.float32).reshape(
        SPAN, local_heads, HEAD_SIZE
    )
    flattened_keys = jnp.dot(
        normalized_rows, key_projection_weight, preferred_element_type=jnp.float32
    ).reshape(SPAN, key_heads, HEAD_SIZE)
    queries = rotate(rms_rows(query_flat, query_gain), positions).astype(jnp.bfloat16)
    queries, first_pages, late = lax.optimization_barrier((queries, first_pages, outgoing[1]))
    second_pages = exchange(late)
    new_keys = rotate(rms_rows(flattened_keys, key_gain), positions).astype(jnp.bfloat16)
    fresh_value_rows = (
        jnp.dot(normalized_rows, value_projection_weight, preferred_element_type=jnp.float32)
        .astype(jnp.bfloat16)
        .reshape(SPAN, key_heads, HEAD_SIZE)
    )
    page_count = SPAN // PAGE_TOKENS
    stacked_pages = jnp.stack([new_keys, fresh_value_rows], axis=2)
    fresh_pages = (
        stacked_pages.reshape(page_count, PAGE_TOKENS, key_heads, 2, HEAD_SIZE)
        .transpose(0, 2, 3, 1, 4)
        .reshape(page_count, key_heads * 2 * PAGE_TOKENS * HEAD_SIZE)
    )
    targets = new_owner[0, :, 0]
    page_index = jnp.arange(page_count, dtype=jnp.int32)
    earlier = page_index[None, :] < page_index[:, None]
    ranks = jnp.sum((targets[:, None] == targets[None, :]) & earlier, axis=1)
    slot_index = jnp.arange(data_ways * NCAP, dtype=jnp.int32)
    selector = ((targets * NCAP + ranks)[None, :] == slot_index[:, None]).astype(jnp.bfloat16)
    outgoing_pages = jnp.dot(selector, fresh_pages, preferred_element_type=jnp.float32).astype(
        jnp.bfloat16
    )
    outgoing_pages = outgoing_pages.reshape(data_ways * NCAP, key_heads, 2, PAGE_TOKENS, HEAD_SIZE)
    outgoing_pages = outgoing_pages.reshape(
        (data_ways, NCAP) + outgoing_pages.shape[1:]
    )
    every = lax.all_gather(outgoing_pages, "dp", axis=0)
    same = own_row[:, None] == own_row[None, :]
    later = jnp.arange(MOST_PAGES)[:, None] > jnp.arange(MOST_PAGES)[None, :]
    page_ranks = jnp.sum(same & later, axis=1).astype(jnp.int32)
    live_tokens = jnp.clip(
        length - jnp.arange(MOST_PAGES, dtype=jnp.int32) * PAGE_TOKENS, 0, PAGE_TOKENS
    )
    everywhere = jnp.stack([own_row, page_ranks])

    def subset(chosen, shift):
        order = jnp.cumsum(chosen.astype(jnp.int32)) - 1
        landed = chosen[:, None] & (order[:, None] == jnp.arange(MOST_PAGES)[None, :])
        table = jnp.stack([own_row, page_ranks - shift])
        table = jnp.sum(jnp.where(landed[None], table[:, :, None], 0), axis=1)
        return (table, jnp.sum(jnp.where(chosen, live_tokens, 0)).reshape(1))

    first_table, first_length = subset(page_ranks < early, 0)
    second_table, second_length = subset(page_ranks >= early, early)
    tensors = (
        queries.reshape(SPAN, local_heads * HEAD_SIZE),
        new_keys.reshape(SPAN, key_heads * HEAD_SIZE),
        fresh_value_rows.reshape(SPAN, key_heads * HEAD_SIZE),
    )
    attn_out = None
    last = key_heads - 1
    for h in range(last):
        attn_out = attend(
            everywhere, prefix_len, *tensors, first_pages, h, key_heads, scale, h * capacity, None, attn_out, True
        )
    if attn_out is not None:
        attn_out, first_length = lax.optimization_barrier((attn_out, first_length))
    state = attend(
        first_table, first_length, *tensors, first_pages, last, key_heads, scale, last * capacity, None, None, False
    )
    every, state = lax.optimization_barrier((every, state))
    fresh_page_store = lax.dynamic_index_in_dim(every, request, 1, keepdims=False)
    fresh_page_store = fresh_page_store.reshape((data_ways * NCAP,) + outgoing_pages.shape[2:])
    attn_out = attend(
        second_table, second_length, *tensors, second_pages, last, key_heads, scale, 0, list(state), attn_out, True
    )
    return (attn_out, fresh_page_store)


def solution(mesh):
    return jax.shard_map(
        shards,
        mesh=mesh,
        in_specs=(
            P("dp", "tensor"),
            P(),
            P(None, "tensor"),
            P(None, "tensor"),
            P(None, "tensor"),
            P(),
            P(),
            P(("dp", "tensor"), None, None, None, None),
            P(),
            P(),
            P("dp"),
            P("dp", None, None),
        ),
        out_specs=(P("dp", "tensor"), P("dp", "tensor", None, None, None)),
        check_vma=False,
    )
```
